512 devices in a mesh: dp: 4 (over z_lo), ctx: 16 (over y, x), tp: 8 (over z_hi, core).
Axes of the slice: x: 4, y: 4, z: 16 (z_hi: 4, z_lo: 4; z = z_hi * 4 + z_lo), core: 2. Of those that a mesh axis runs over, the one named last changes fastest.
Arguments:
- query_b: bfloat16 [8192, 8192], P(('dp', 'ctx'), 'tp'), parts along dimension 0, may hold values from -6 to 6
- key_b: bfloat16 [8192, 8192], P(('dp', 'ctx'), 'tp'), parts along dimension 0, may hold values from -6 to 6
- value_b: bfloat16 [8192, 8192], P(('dp', 'ctx'), 'tp'), parts along dimension 0, may hold values from -6 to 6
- filter_b: bfloat16 [2048, 8192], P('ctx', 'tp'), may hold values from -6 to 6
- skip_b: bfloat16 [8192], P('tp'), may hold values from 0.5 to 1.5
- acts_a: bfloat16 [2048, 8192], P(('dp', 'tp'), 'ctx'), parts along dimension 0, may hold values from -1800 to 1800
- gain_a: float32 [8192], P('ctx'), may hold values from 0.1 to 1.9
- w_gate: bfloat16 [8192, 11264], P('ctx', 'tp'), may hold values from -0.0625 to 0.0625
- w_up: bfloat16 [8192, 11264], P('ctx', 'tp'), may hold values from -0.0625 to 0.0625
- grad_hidden: bfloat16 [2048, 11264], P(('dp', 'ctx'), 'tp'), parts along dimension 0, may hold values from -6 to 6
Outputs:
- gated: bfloat16 [8192, 8192], P(('dp', 'ctx'), 'tp'), parts along dimension 0
- grad_gate: bfloat16 [2048, 11264], P(('dp', 'ctx'), 'tp'), parts along dimension 0
- grad_up: bfloat16 [2048, 11264], P(('dp', 'ctx'), 'tp'), parts along dimension 0
The draws below stay inside these ranges and needn't reach their ends.
There are 4 independent parts, one for each index of `dp`. The reference program is written for one: setup_inputs(seed, part) draws one part's arguments, and reference() takes and returns one part's arrays. A program takes and returns all parts, laid end to end along the dimension named above; an argument that names none is the same for every part. Nothing has to cross between parts.
All inputs are finite; a program needn't handle non-finite values.
Results may differ from the reference program's by a relative error of at most 0.0053.
Values may be sent and summed in bfloat16 or wider, within the bound.
A program may use at most 64 MiB of HBM per device.

```python
import math
import jax
import jax.numpy as jnp
from jax import lax

D = 8192
FFW = 11264
LENGTH = 2048
TOKENS_A = 512


def draw_filter_b(key, part):
    key = jax.random.fold_in(key, 11)
    rate_key, tap_key = jax.random.split(key)
    log_rate = jax.random.uniform(rate_key, (D,), jnp.float32, math.log(0.5 / LENGTH), math.log(0.05))
    taps = jnp.clip(jax.random.normal(tap_key, (LENGTH, D), jnp.float32), -6.0, 6.0)
    rate = jnp.exp(log_rate)[None, :]
    lags = jnp.arange(LENGTH, dtype=jnp.float32)[:, None]
    envelope = jnp.exp(-rate * lags) * jnp.sqrt(1.0 - jnp.exp(-2.0 * rate))
    return (taps * envelope).astype(jnp.bfloat16)


def draw_acts_a(key, part):
    key = jax.random.fold_in(key, 23)
    base_key, col_key, row_key = jax.random.split(key, 3)
    columns = jnp.arange(D, dtype=jnp.float32) / D
    col_scale = jnp.exp(columns * math.log(3.0) + jax.random.uniform(col_key, (D,), jnp.float32, 0.0, math.log(10.0)))
    row_scale = jnp.exp(jax.random.uniform(row_key, (TOKENS_A, 1), jnp.float32, 0.0, math.log(10.0)))
    base = jnp.clip(jax.random.normal(base_key, (TOKENS_A, D), jnp.float32), -6.0, 6.0)
    return (base * row_scale * col_scale[None, :]).astype(jnp.bfloat16)


def steps_of(own_key, extent, shards, smallest, top_value):
    def one(dim, parts):
        steps = jax.random.uniform(jax.random.fold_in(jax.random.fold_in(own_key, 6), dim), (parts,), jnp.float32, smallest / len(shards), top_value / len(shards))
        return jnp.repeat(jnp.exp(steps), extent[dim] // parts).reshape((-1,) + (1,) * (len(extent) - dim - 1))

    loudness = one(*shards[0])
    for cut in shards[1:]:
        loudness = loudness * one(*cut)
    return loudness


def normal_values(key, extent, spread, most, cuts=(), kind=jnp.bfloat16):
    drawn = spread * jax.random.normal(key, extent, jnp.float32)
    if cuts:
        drawn = drawn * steps_of(key, extent, cuts, -0.22, 0.18)
    return jnp.clip(drawn, -most, most).astype(kind)


def setup_inputs(seed: int = 0, part: int = 0) -> dict:
    keys = jax.random.split(jax.random.key(seed), 11)
    part_splits = jax.random.split(jax.random.fold_in(keys[10], part), 11)
    return {
        "query_b": normal_values(part_splits[0], (LENGTH, D), 1.0, 6.0, ((0, 16), (1, 8))),
        "key_b": normal_values(part_splits[1], (LENGTH, D), 1.0, 6.0, ((0, 16), (1, 8))),
        "value_b": normal_values(part_splits[2], (LENGTH, D), 1.0, 6.0, ((0, 16), (1, 8))),
        "filter_b": draw_filter_b(jax.random.fold_in(keys[10], 71), part),
        "skip_b": jnp.clip(0.5 + 1.0 * jax.random.uniform(keys[4], (D,), jnp.float32) ** steps_of(keys[4], (D,), ((0, 8),), -0.2, 0.2), 0.5, 1.5).astype(jnp.bfloat16),
        "acts_a": draw_acts_a(jax.random.fold_in(jax.random.fold_in(keys[10], part), 71), part),
        "gain_a": jnp.clip(1.0 + 0.18 * jax.random.normal(keys[6], (D,), jnp.float32), 0.1, 1.9),
        "w_gate": normal_values(keys[7], (D, FFW), D ** -0.5, 0.0625, ((0, 16), (1, 8))),
        "w_up": normal_values(keys[8], (D, FFW), D ** -0.5, 0.0625, ((0, 16), (1, 8))),
        "grad_hidden": normal_values(part_splits[9], (TOKENS_A, FFW), 1.0, 6.0, ((0, 16), (1, 8))),
    }


def reference(query_b, key_b, value_b, filter_b, skip_b, acts_a, gain_a, w_gate, w_up, grad_hidden):
    mixed = (key_b.astype(jnp.float32) * value_b.astype(jnp.float32)).astype(jnp.bfloat16)
    length = mixed.shape[0]
    period = 2 * length
    signal_freq = jnp.fft.rfft(mixed.astype(jnp.float32), n=period, axis=0)
    filter_freq = jnp.fft.rfft(filter_b.astype(jnp.float32), n=period, axis=0)
    conv = jnp.fft.irfft(signal_freq * filter_freq, n=period, axis=0)[:length]
    conv = lax.optimization_barrier(conv.astype(jnp.bfloat16)).astype(jnp.float32)
    direct = skip_b.astype(jnp.float32)[None, :] * mixed.astype(jnp.float32)
    gated = (query_b.astype(jnp.float32) * (conv + direct)).astype(jnp.bfloat16)
    rows = acts_a.astype(jnp.float32)
    power = lax.optimization_barrier(jnp.mean(rows * rows, axis=1, keepdims=True))
    normed = (rows * lax.rsqrt(power + 1e-06) * gain_a[None, :]).astype(jnp.bfloat16)
    gate = jnp.dot(normed, w_gate, preferred_element_type=jnp.float32)
    up_part = jnp.dot(normed, w_up, preferred_element_type=jnp.float32)
    sigma = jax.nn.sigmoid(gate)
    upstream = grad_hidden.astype(jnp.float32)
    grad_gate = (upstream * up_part * sigma * (1.0 + gate * (1.0 - sigma))).astype(jnp.bfloat16)
    grad_up = (upstream * gate * sigma).astype(jnp.bfloat16)
    return (gated, grad_gate, grad_up)
```

```python
import functools
import math

import jax
import jax.numpy as jnp
import numpy as np
from jax import lax
from jax.experimental import pallas as pl
from jax.experimental.pallas import tpu as pltpu
from jax.sharding import PartitionSpec as P

D = 8192
EPSILON = 1e-06
SIDE = 4
GROUP = 16
BLOCK = 256
CHUNKS = (384, 384, 384, 256)
STARTS = tuple(sum(CHUNKS[:i]) for i in range(len(CHUNKS)))
MESH = pl.DeviceIdType.MESH
F32 = jnp.float32
BF16 = jnp.bfloat16


def dft_tables():
    order = np.concatenate((np.arange(0, BLOCK, 2), np.arange(1, BLOCK, 2)))
    angle = np.outer(2 * order + 1, np.arange(BLOCK)) % (4 * BLOCK)
    angle = angle.astype(np.float64) * (math.pi / (2 * BLOCK))
    full = np.concatenate((np.cos(angle), -np.sin(angle)), axis=0)
    high = full.astype(jnp.bfloat16)
    low = (full - high.astype(np.float64)).astype(jnp.bfloat16)
    back = np.ascontiguousarray((full.T / BLOCK)).astype(jnp.bfloat16)
    return high, low, back


def kernel(
    query_h, key_h, value_h, taps_h, skip_ref, acts_h, gain_ref, wg_h, wu_h, grad_h,
    high_h, low_h, back_h,
    gated_ref, gg_ref, gu_ref,
    query, key, value, taps, wg, wu, grad, high, low, back,
    mixed, send_u, recv_u, spec, turned, joint, send_c, recv_c,
    rows, scaled, send_q, recv_q, spread,
    *rest,
):
    n = len(CHUNKS)
    parts = (rest[0:n], rest[n:2 * n])
    got1p, got1m, got2p, got2m, sums, got3p, got3m, got4p, got4m = (
        (rest[(2 + 2 * i) * n:(3 + 2 * i) * n], rest[(3 + 2 * i) * n:(4 + 2 * i) * n])
        for i in range(9)
    )
    (load_sem, u_send, u_recv, c_send, c_recv, q_send, q_recv, z_send, z_recv,
     r_send, r_recv) = rest[20 * n:]

    ctx = lax.axis_index("ctx")
    tp = lax.axis_index("tp")
    y, x = lax.div(ctx, SIDE), lax.rem(ctx, SIDE)
    z, core = lax.div(tp, 2), lax.rem(tp, 2)

    def turn(value_, by):
        return lax.rem(value_ + by, SIDE)

    left = turn(z, 3) * 2 + core
    right = turn(z, 1) * 2 + core
    far = turn(z, 2) * 2 + core
    other = z * 2 + 1 - core

    loads = {}
    for i, (name, src, dst) in enumerate((
        ("key", key_h, key), ("value", value_h, value), ("taps", taps_h, taps),
        ("acts", acts_h, rows.at[tp]), ("high", high_h, high), ("low", low_h, low),
        ("wg", wg_h, wg), ("wu", wu_h, wu), ("back", back_h, back),
        ("query", query_h, query), ("grad", grad_h, grad),
    )):
        loads[name] = pltpu.make_async_copy(src, dst, load_sem.at[i])
        loads[name].start()

    barrier = pltpu.get_barrier_semaphore()

    @pl.loop(1, GROUP)
    def _(k):
        pl.semaphore_signal(
            barrier, inc=1, device_id={"ctx": lax.rem(ctx + k, GROUP)}, device_id_type=MESH)

    for peer in (left, right, other):
        pl.semaphore_signal(barrier, inc=1, device_id={"tp": peer}, device_id_type=MESH)

    lane = lax.broadcasted_iota(jnp.int32, (128, 128), 1)
    low_half = lane < 64

    for name in ("key", "value", "taps"):
        loads[name].wait()

    @pl.loop(0, GROUP // 2)
    def _(i):
        at = pl.ds(pl.multiple_of(i * 128, 128), 128)
        signal = (key[:, at].astype(F32) * value[:, at].astype(F32)).astype(BF16)
        mixed[:, at] = signal
        signal = signal.astype(F32)
        lags = taps[:, at].astype(F32)
        send_u[2 * i] = jnp.where(low_half, signal, pltpu.roll(lags, 64, 1)).astype(BF16)
        send_u[2 * i + 1] = jnp.where(low_half, pltpu.roll(signal, 64, 1), lags).astype(BF16)

    pl.semaphore_wait(barrier, GROUP + 2)

    def z_copy(i, block, half, peer, whole=False):
        at = rows.at[block] if whole else rows.at[block, pl.ds(32 * half, 32)]
        return pltpu.make_async_remote_copy(
            src_ref=at, dst_ref=at, send_sem=z_send.at[i], recv_sem=z_recv.at[i],
            device_id={"tp": peer}, device_id_type=MESH)

    loads["acts"].wait()
    own = [
        z_copy(0, tp, 0, right), z_copy(1, tp, 1, left),
        z_copy(2, tp, 1, right), z_copy(3, tp, 0, left),
        z_copy(4, tp, 0, other, whole=True),
    ]
    for copy in own:
        copy.start()

    def exchange(src, dst, send_sem, recv_sem, pick=lambda peer: peer):
        def one(k):
            peer = lax.rem(ctx + k, GROUP)
            return pltpu.make_async_remote_copy(
                src_ref=src.at[pick(peer)], dst_ref=dst.at[ctx],
                send_sem=send_sem.at[peer], recv_sem=recv_sem.at[ctx],
                device_id={"ctx": peer}, device_id_type=MESH)

        def arrival(k):
            peer = lax.rem(ctx + k, GROUP)
            return pltpu.make_async_remote_copy(
                src_ref=src.at[pick(peer)], dst_ref=dst.at[peer],
                send_sem=send_sem.at[peer], recv_sem=recv_sem.at[peer],
                device_id={"ctx": peer}, device_id_type=MESH)

        def start():
            @pl.loop(1, GROUP)
            def _(k):
                one(k).start()

        def wait_recv():
            @pl.loop(1, GROUP)
            def _(k):
                arrival(k).wait_recv()

        def wait_send():
            @pl.loop(1, GROUP)
            def _(k):
                one(k).wait_send()

        return start, wait_recv, wait_send

    u_start, u_wait, u_drain = exchange(send_u, recv_u, u_send, u_recv)
    c_start, c_wait, c_drain = exchange(send_c, recv_c, c_send, c_recv)
    q_start, q_wait, q_drain = exchange(
        send_q, recv_q, q_send, q_recv, lambda peer: lax.div(peer, SIDE))
    u_start()
    recv_u[ctx] = send_u[ctx]

    z_copy(0, left, 0, right).wait_recv()
    ahead = z_copy(5, left, 0, right)
    ahead.start()
    z_copy(1, right, 1, left).wait_recv()
    behind = z_copy(6, right, 1, left)
    behind.start()
    passed = [z_copy(7, left, 0, other), z_copy(8, right, 1, other)]
    passed[0].start()
    passed[1].start()
    z_copy(2, left, 1, right).wait_recv()
    passed.append(z_copy(9, left, 1, other))
    passed[2].start()
    z_copy(3, right, 0, left).wait_recv()
    passed.append(z_copy(10, right, 0, other))
    passed[3].start()

    u_wait()
    loads["high"].wait()
    loads["low"].wait()

    @pl.loop(0, 4)
    def _(i):
        pair = jnp.concatenate(
            (recv_u[pl.ds(4 * i, 2)].reshape(BLOCK, 128),
             recv_u[pl.ds(4 * i + 2, 2)].reshape(BLOCK, 128)), axis=1)
        result = jnp.dot(high[...], pair, preferred_element_type=F32)
        result += jnp.dot(low[...], pair, preferred_element_type=F32)
        for h in range(2):
            half = result[:, 128 * h:128 * h + 128]
            spec[2 * i + h] = half
            turned[2 * i + h] = pltpu.roll(half, 64, 1)

    @pl.loop(0, 16)
    def _(r):
        re = pl.ds(pl.multiple_of(16 * r, 16), 16)
        im = pl.ds(pl.multiple_of(BLOCK + 16 * r, 16), 16)
        sign = 1.0 - 2.0 * lax.div(r, 8).astype(F32)
        last = None
        for i in range(8):
            total_re = total_im = None
            for a in range(i // 2 + 1):
                b = i - a
                a_re, a_im = spec[a, re], spec[a, im]
                b_re, b_im = turned[b, re], turned[b, im]
                one_re = a_re * b_re - a_im * b_im
                one_im = a_re * b_im + a_im * b_re
                if a == b:
                    one_re, one_im = 0.5 * one_re, 0.5 * one_im
                total_re = one_re if total_re is None else total_re + one_re
                total_im = one_im if total_im is None else total_im + one_im
            if last is None:
                joint[i, re] = total_re.astype(BF16)
                joint[i, im] = total_im.astype(BF16)
            else:
                joint[i, re] = (total_re - sign * last[1]).astype(BF16)
                joint[i, im] = (total_im + sign * last[0]).astype(BF16)
            last = (total_re, total_im)

    loads["back"].wait()

    @pl.loop(0, 4)
    def _(i):
        pair = jnp.concatenate((joint[2 * i], joint[2 * i + 1]), axis=1)
        result = jnp.dot(back[...], pair, preferred_element_type=F32)
        for h in range(2):
            half = result[:, 128 * h:128 * h + 128]
            half = half + pltpu.roll(half, 64, 1)
            for d in range(2):
                send_c[4 * i + 2 * h + d] = jnp.where(
                    low_half[:64], half[128 * d:128 * d + 64], half[128 * d + 64:128 * d + 128]
                ).astype(BF16)

    c_start()
    recv_c[ctx] = send_c[ctx]

    z_copy(5, far, 0, right).wait_recv()
    passed.append(z_copy(11, far, 0, other))
    passed[4].start()
    z_copy(6, far, 1, left).wait_recv()
    passed.append(z_copy(12, far, 1, other))
    passed[5].start()
    mate = 1 - core
    z_copy(4, other, 0, other, whole=True).wait_recv()
    for i, block, half in (
        (7, turn(z, 3), 0), (8, turn(z, 1), 1), (9, turn(z, 3), 1), (10, turn(z, 1), 0),
        (11, turn(z, 2), 0), (12, turn(z, 2), 1),
    ):
        z_copy(i, block * 2 + mate, half, other).wait_recv()

    @pl.loop(0, SIDE)
    def _(i):
        block = rows[pl.ds(2 * i, 2)].reshape(128, 512).astype(F32)
        squares = block * block
        squares = (squares[:, :128] + squares[:, 128:256]) + (
            squares[:, 256:384] + squares[:, 384:])
        send_q[i] = jnp.broadcast_to(
            jnp.sum(squares.T, axis=0, keepdims=True), (8, 128))
        scaled[pl.ds(pl.multiple_of(128 * i, 128), 128)] = (
            block * gain_ref[...]).astype(BF16)

    q_start()
    recv_q[ctx] = send_q[y]

    first = (x, y)
    second = (y, x)

    def place(g, step, by):
        along_x = (g == 0) == (step == 0)
        return turn(x, by) + SIDE * y if along_x else x + SIDE * turn(y, by)

    def r_copy(g, c, kind, src, dst, by):
        i = (g * n + c) * 8 + kind
        return pltpu.make_async_remote_copy(
            src_ref=src, dst_ref=dst, send_sem=r_send.at[i], recv_sem=r_recv.at[i],
            device_id={"ctx": place(g, 0 if kind < 4 else 1, by)}, device_id_type=MESH)

    def link(g, c, kind):
        part, f, s = parts[g][c], first[g], second[g]
        total = sums[g][c]
        if kind == 0:
            return r_copy(g, c, 0, part.at[turn(f, 2), pl.ds(0, 2)], got1p[g][c], 1)
        if kind == 1:
            return r_copy(g, c, 1, part.at[turn(f, 2), pl.ds(2, 2)], got1m[g][c], 3)
        if kind == 2:
            return r_copy(g, c, 2, part.at[turn(f, 1)], got2p[g][c], 1)
        if kind == 3:
            return r_copy(g, c, 3, part.at[turn(f, 3)], got2m[g][c], 3)
        if kind == 4:
            return r_copy(g, c, 4, total.at[turn(s, 2), pl.ds(0, 16)], got3p[g][c], 1)
        if kind == 5:
            return r_copy(g, c, 5, total.at[turn(s, 2), pl.ds(16, 16)], got3m[g][c], 3)
        if kind == 6:
            return r_copy(g, c, 6, total.at[turn(s, 1)], got4p[g][c], 1)
        return r_copy(g, c, 7, total.at[turn(s, 3)], got4m[g][c], 3)

    weights = (wg, wu)
    loads["wg"].wait()
    loads["wu"].wait()

    def step1(g, c):
        width = CHUNKS[c]
        part = parts[g][c]

        @pl.loop(0, 2)
        def _(i):
            result = jnp.dot(
                scaled[pl.ds(pl.multiple_of(256 * i, 256), 256)],
                weights[g][:, STARTS[c]:STARTS[c] + width], preferred_element_type=F32)
            for b in range(8):
                block = result[32 * b:32 * b + 32].astype(BF16)
                row, col = 2 * i + b // 4, b % 4
                if g == 0:
                    part[col, row] = block
                else:
                    part[row, col] = block

        link(g, c, 0).start()
        link(g, c, 1).start()

    def add(into, index, value_):
        into[index] = (into[index].astype(F32) + value_.astype(F32)).astype(BF16)

    def step2(g, c):
        part, f = parts[g][c], first[g]
        link(g, c, 0).wait_recv()
        for b in range(2):
            add(part, (turn(f, 1), b), got1p[g][c][b])
        link(g, c, 2).start()
        link(g, c, 1).wait_recv()
        for b in range(2):
            add(part, (turn(f, 3), 2 + b), got1m[g][c][b])
        link(g, c, 3).start()

    def step3(g, c):
        part, f = parts[g][c], first[g]
        link(g, c, 2).wait_recv()
        link(g, c, 3).wait_recv()
        for b in range(SIDE):
            sums[g][c][b] = (
                part[f, b].astype(F32) + got2p[g][c][b].astype(F32)
                + got2m[g][c][b].astype(F32)).astype(BF16)
        link(g, c, 4).start()
        link(g, c, 5).start()

    def step4(g, c):
        total, s = sums[g][c], second[g]
        link(g, c, 4).wait_recv()
        add(total, (turn(s, 1), pl.ds(0, 16)), got3p[g][c][...])
        link(g, c, 6).start()
        link(g, c, 5).wait_recv()
        add(total, (turn(s, 3), pl.ds(16, 16)), got3m[g][c][...])
        link(g, c, 7).start()

    def finish(c, scale):
        values = []
        for g in range(2):
            link(g, c, 6).wait_recv()
            link(g, c, 7).wait_recv()
            total = (sums[g][c][second[g]].astype(F32) + got4p[g][c][...].astype(F32)
                     + got4m[g][c][...].astype(F32))
            values.append(total * scale)
        gate, up = values
        at = slice(STARTS[c], STARTS[c] + CHUNKS[c])
        sigma = jax.nn.sigmoid(gate)
        upstream = grad[:, at].astype(F32)
        gg_ref[:, at] = (upstream * up * sigma * (1.0 + gate * (1.0 - sigma))).astype(BF16)
        gu_ref[:, at] = (upstream * gate * sigma).astype(BF16)

    for c in range(n):
        for g in range(2):
            step1(g, c)

    for c in range(n + 2):
        if c < n:
            step2(0, c)
            step2(1, c)
        if 0 <= c - 1 < n:
            step3(0, c - 1)
            step3(1, c - 1)
        if 0 <= c - 2 < n:
            step4(0, c - 2)
            step4(1, c - 2)
        if c == 1:
            c_wait()
            loads["query"].wait()

            @pl.loop(0, GROUP // 2)
            def _(i):
                at = pl.ds(pl.multiple_of(i * 128, 128), 128)
                even = recv_c[2 * i].astype(F32)
                odd = recv_c[2 * i + 1].astype(F32)
                conv = jnp.concatenate(
                    (jnp.where(low_half[:64], even, pltpu.roll(odd, 64, 1)),
                     jnp.where(low_half[:64], pltpu.roll(even, 64, 1), odd)), axis=0)
                direct = skip_ref[:, at].astype(F32) * mixed[:, at].astype(F32)
                gated_ref[:, at] = (
                    query[:, at].astype(F32) * (conv + direct)).astype(BF16)

    q_wait()
    power = recv_q[0]
    for i in range(1, GROUP):
        power = power + recv_q[i]
    spread[...] = jnp.broadcast_to(power[0:1], (128, 128)).T
    mine = spread[pl.ds(pl.multiple_of(32 * x, 32), 32), :]
    scale = lax.rsqrt(mine[:, :1] / D + EPSILON)
    loads["grad"].wait()
    for c in range(n):
        finish(c, scale)

    u_drain()
    c_drain()
    q_drain()
    for copy in own + [ahead, behind] + passed:
        copy.wait_send()
    for g in range(2):
        for c in range(n):
            for kind in range(8):
                link(g, c, kind).wait_send()


def body(query_b, key_b, value_b, filter_b, skip_b, acts_a, gain_a, w_gate, w_up, grad_hidden):
    high, low, back = dft_tables()
    any_spec = pl.BlockSpec(memory_space=pl.ANY)
    vmem = pl.BlockSpec(memory_space=pltpu.VMEM)
    length, width = key_b.shape
    hidden = w_gate.shape[1]

    def per_chunk(*lead):
        return [pltpu.VMEM(lead + (w,), BF16) for w in CHUNKS] * 2

    scratch = [
        pltpu.VMEM((length, width), BF16),
        pltpu.VMEM((length, width), BF16),
        pltpu.VMEM((length, width), BF16),
        pltpu.VMEM((length, width), BF16),
        pltpu.VMEM(w_gate.shape, BF16),
        pltpu.VMEM(w_up.shape, BF16),
        pltpu.VMEM(grad_hidden.shape, BF16),
        pltpu.VMEM(high.shape, BF16),
        pltpu.VMEM(low.shape, BF16),
        pltpu.VMEM(back.shape, BF16),
        pltpu.VMEM((length, width), BF16),
        pltpu.VMEM((GROUP, 128, 128), BF16),
        pltpu.VMEM((GROUP, 128, 128), BF16),
        pltpu.VMEM((8, 2 * BLOCK, 128), F32),
        pltpu.VMEM((8, 2 * BLOCK, 128), F32),
        pltpu.VMEM((8, 2 * BLOCK, 128), BF16),
        pltpu.VMEM((GROUP, 64, 128), BF16),
        pltpu.VMEM((GROUP, 64, 128), BF16),
        pltpu.VMEM((8, 64, 512), BF16),
        pltpu.VMEM((512, 512), BF16),
        pltpu.VMEM((SIDE, 8, 128), F32),
        pltpu.VMEM((GROUP, 8, 128), F32),
        pltpu.VMEM((128, 128), F32),
    ]
    scratch += per_chunk(SIDE, SIDE, 32)
    scratch += per_chunk(2, 32) + per_chunk(2, 32)
    scratch += per_chunk(SIDE, 32) + per_chunk(SIDE, 32)
    scratch += per_chunk(SIDE, 32)
    scratch += per_chunk(16) + per_chunk(16)
    scratch += per_chunk(32) + per_chunk(32)
    links = 2 * len(CHUNKS) * 8
    for size in (11, GROUP, GROUP, GROUP, GROUP, GROUP, GROUP, 13, 13, links, links):
        scratch.append(pltpu.SemaphoreType.DMA((size,)))
    return pl.pallas_call(
        kernel,
        out_shape=(
            jax.ShapeDtypeStruct((length, width), BF16),
            jax.ShapeDtypeStruct(grad_hidden.shape, BF16),
            jax.ShapeDtypeStruct(grad_hidden.shape, BF16),
        ),
        in_specs=[any_spec] * 4 + [vmem, any_spec, vmem] + [any_spec] * 6,
        out_specs=(vmem, vmem, vmem),
        scratch_shapes=scratch,
        compiler_params=pltpu.CompilerParams(
            collective_id=0, has_side_effects=True, vmem_limit_bytes=56 * 1024 * 1024),
        name="hyena",
    )(
        query_b, key_b, value_b, filter_b, skip_b.reshape(1, -1), acts_a,
        gain_a.reshape(1, -1), w_gate, w_up, grad_hidden,
        jnp.asarray(high), jnp.asarray(low), jnp.asarray(back),
    )


def solution(mesh):
    return jax.shard_map(
        body,
        mesh=mesh,
        in_specs=(
            P(("dp", "ctx"), "tp"),
            P(("dp", "ctx"), "tp"),
            P(("dp", "ctx"), "tp"),
            P("ctx", "tp"),
            P("tp"),
            P(("dp", "tp"), "ctx"),
            P("ctx"),
            P("ctx", "tp"),
            P("ctx", "tp"),
            P(("dp", "ctx"), "tp"),
        ),
        out_specs=(P(("dp", "ctx"), "tp"), P(("dp", "ctx"), "tp"), P(("dp", "ctx"), "tp")),
        check_vma=False,
    )
```

```python
import math

import jax
import jax.numpy as jnp
import numpy as np
from jax import lax
from jax.experimental import pallas as pl
from jax.experimental.pallas import tpu as pltpu
from jax.sharding import PartitionSpec as P

D = 8192
EPSILON = 1e-06
SIDE = 4
GROUP = 16
BLOCK = 256
CHUNKS = (384, 384, 384, 256)
STARTS = tuple(sum(CHUNKS[:i]) for i in range(len(CHUNKS)))
MESH = pl.DeviceIdType.MESH
F32 = jnp.float32
BF16 = jnp.bfloat16


def dft_tables():
    order = np.concatenate((np.arange(0, BLOCK, 2), np.arange(1, BLOCK, 2)))
    angle = np.outer(2 * order + 1, np.arange(BLOCK)) % (4 * BLOCK)
    angle = angle.astype(np.float64) * (math.pi / (2 * BLOCK))
    full = np.concatenate((np.cos(angle), -np.sin(angle)), axis=0)
    high = full.astype(jnp.bfloat16)
    low = (full - high.astype(np.float64)).astype(jnp.bfloat16)
    back = np.ascontiguousarray((full.T / BLOCK)).astype(jnp.bfloat16)
    return high, low, back


def kernel(
    query_h, key_h, value_h, taps_h, skip_ref, acts_h, gain_ref, wg_h, wu_h,
    high_h, low_h, back_h,
    gated_ref, gate_ref, up_ref,
    query, key, value, taps, wg, wu, high, low, back,
    mixed, send_u, recv_u, spec, turned, joint, send_c, recv_c,
    rows, scaled, send_q, recv_q, spread,
    *rest,
):
    n = len(CHUNKS)
    (parts, s1_out, s1p_in, s1m_in, s2p_out, s2m_out, s2p_in, s2m_in,
     t1_out, t1p_in, t1m_in, t2p_out, t2m_out, t2p_in, t2m_in) = (
        (rest[2 * i * n:(2 * i + 1) * n], rest[(2 * i + 1) * n:(2 * i + 2) * n])
        for i in range(15)
    )
    t0_in = rest[30 * n:30 * n + 2]
    (load_sem, u_send, u_recv, c_send, c_recv, q_send, q_recv, z_send, z_recv,
     r_send, r_recv) = rest[30 * n + 2:]

    ctx = lax.axis_index("ctx")
    tp = lax.axis_index("tp")
    y, x = lax.div(ctx, SIDE), lax.rem(ctx, SIDE)
    z, core = lax.div(tp, 2), lax.rem(tp, 2)

    def turn(value_, by):
        return lax.rem(value_ + by, SIDE)

    left = turn(z, 3) * 2 + core
    right = turn(z, 1) * 2 + core
    far = turn(z, 2) * 2 + core
    other = z * 2 + 1 - core
    left_mate, right_mate = turn(z, 3) * 2 + 1 - core, turn(z, 1) * 2 + 1 - core

    barrier = pltpu.get_barrier_semaphore()

    @pl.loop(1, GROUP)
    def _(k):
        pl.semaphore_signal(
            barrier, inc=1, device_id={"ctx": lax.rem(ctx + k, GROUP)}, device_id_type=MESH)

    for peer in (left, right, other, left_mate, right_mate):
        pl.semaphore_signal(barrier, inc=1, device_id={"tp": peer}, device_id_type=MESH)

    loads = {}
    for i, (name, src, dst) in enumerate((
        ("key", key_h, key), ("value", value_h, value), ("taps", taps_h, taps),
        ("acts", acts_h, rows.at[tp]), ("high", high_h, high), ("low", low_h, low),
        ("wg", wg_h, wg), ("wu", wu_h, wu), ("back", back_h, back),
        ("query", query_h, query),
    )):
        loads[name] = pltpu.make_async_copy(src, dst, load_sem.at[i])
        loads[name].start()

    lane = lax.broadcasted_iota(jnp.int32, (128, 128), 1)
    low_half = lane < 64

    pl.semaphore_wait(barrier, GROUP + 4)

    def z_copy(i, block, half, peer, whole=False, first=False):
        part = pl.ds(0, 64) if whole else pl.ds(32 * half, 32)
        at = rows.at[block, part]
        return pltpu.make_async_remote_copy(
            src_ref=acts_h.at[part] if first else at, dst_ref=at,
            send_sem=z_send.at[i], recv_sem=z_recv.at[i],
            device_id={"tp": peer}, device_id_type=MESH)

    own = [
        z_copy(0, tp, 0, right, first=True), z_copy(1, tp, 1, left, first=True),
        z_copy(4, tp, 0, other, whole=True, first=True),
        z_copy(2, tp, 1, right, first=True), z_copy(3, tp, 0, left, first=True),
    ]
    for copy in own[:3]:
        copy.start()

    for name in ("key", "value", "taps"):
        loads[name].wait()

    @pl.loop(0, GROUP // 2)
    def _(i):
        at = pl.ds(pl.multiple_of(i * 128, 128), 128)
        signal = (key[:, at].astype(F32) * value[:, at].astype(F32)).astype(BF16)
        mixed[:, at] = signal
        signal = signal.astype(F32)
        lags = taps[:, at].astype(F32)
        send_u[2 * i] = jnp.where(low_half, signal, pltpu.roll(lags, 64, 1)).astype(BF16)
        send_u[2 * i + 1] = jnp.where(low_half, pltpu.roll(signal, 64, 1), lags).astype(BF16)

    for copy in own[3:]:
        copy.start()

    def exchange(src, dst, send_sem, recv_sem):
        def one(k):
            peer = lax.rem(ctx + k, GROUP)
            return pltpu.make_async_remote_copy(
                src_ref=src.at[peer], dst_ref=dst.at[ctx],
                send_sem=send_sem.at[peer], recv_sem=recv_sem.at[ctx],
                device_id={"ctx": peer}, device_id_type=MESH)

        def arrival(k):
            peer = lax.rem(ctx + k, GROUP)
            return pltpu.make_async_remote_copy(
                src_ref=src.at[peer], dst_ref=dst.at[peer],
                send_sem=send_sem.at[peer], recv_sem=recv_sem.at[peer],
                device_id={"ctx": peer}, device_id_type=MESH)

        def start():
            @pl.loop(1, GROUP)
            def _(k):
                one(k).start()

        def wait_recv():
            @pl.loop(1, GROUP)
            def _(k):
                arrival(k).wait_recv()

        def wait_send():
            @pl.loop(1, GROUP)
            def _(k):
                one(k).wait_send()

        return start, wait_recv, wait_send

    u_start, u_wait, u_drain = exchange(send_u, recv_u, u_send, u_recv)
    c_start, c_wait, c_drain = exchange(send_c, recv_c, c_send, c_recv)
    u_start()
    recv_u[ctx] = send_u[ctx]

    def convolve():
        u_wait()
        loads["high"].wait()
        loads["low"].wait()

        @pl.loop(0, 4)
        def _(i):
            pair = jnp.concatenate(
                (recv_u[pl.ds(4 * i, 2)].reshape(BLOCK, 128),
                 recv_u[pl.ds(4 * i + 2, 2)].reshape(BLOCK, 128)), axis=1)
            result = jnp.dot(high[...], pair, preferred_element_type=F32)
            result += jnp.dot(low[...], pair, preferred_element_type=F32)
            for h in range(2):
                half = result[:, 128 * h:128 * h + 128]
                spec[2 * i + h] = half
                turned[2 * i + h] = pltpu.roll(half, 64, 1)

        @pl.loop(0, 16)
        def _(r):
            re = pl.ds(pl.multiple_of(16 * r, 16), 16)
            im = pl.ds(pl.multiple_of(BLOCK + 16 * r, 16), 16)
            sign = 1.0 - 2.0 * lax.div(r, 8).astype(F32)
            last = None
            for i in range(8):
                total_re = total_im = None
                for a in range(i // 2 + 1):
                    b = i - a
                    a_re, a_im = spec[a, re], spec[a, im]
                    b_re, b_im = turned[b, re], turned[b, im]
                    one_re = a_re * b_re - a_im * b_im
                    one_im = a_re * b_im + a_im * b_re
                    if a == b:
                        one_re, one_im = 0.5 * one_re, 0.5 * one_im
                    total_re = one_re if total_re is None else total_re + one_re
                    total_im = one_im if total_im is None else total_im + one_im
                if last is None:
                    joint[i, re] = total_re.astype(BF16)
                    joint[i, im] = total_im.astype(BF16)
                else:
                    joint[i, re] = (total_re - sign * last[1]).astype(BF16)
                    joint[i, im] = (total_im + sign * last[0]).astype(BF16)
                last = (total_re, total_im)

        loads["back"].wait()

        @pl.loop(0, 4)
        def _(i):
            pair = jnp.concatenate((joint[2 * i], joint[2 * i + 1]), axis=1)
            result = jnp.dot(back[...], pair, preferred_element_type=F32)
            for h in range(2):
                half = result[:, 128 * h:128 * h + 128]
                half = half + pltpu.roll(half, 64, 1)
                for d in range(2):
                    send_c[4 * i + 2 * h + d] = jnp.where(
                        low_half[:64], half[128 * d:128 * d + 64], half[128 * d + 64:128 * d + 128]
                    ).astype(BF16)


    weights = (wg, wu)
    offsets = (0, 3, 1, 2)

    def q_copy(g, by):
        peer = SIDE * g + turn(x, by)
        return pltpu.make_async_remote_copy(
            src_ref=send_q.at[g], dst_ref=recv_q.at[ctx],
            send_sem=q_send.at[peer], recv_sem=q_recv.at[ctx],
            device_id={"ctx": peer}, device_id_type=MESH)

    def prepare(k):
        g = turn(z, offsets[k])
        block = rows[pl.ds(2 * g, 2)].reshape(128, 512).astype(F32)
        squares = block * block
        squares = (squares[:, :128] + squares[:, 128:256]) + (
            squares[:, 256:384] + squares[:, 384:])
        send_q[g] = jnp.broadcast_to(jnp.sum(squares.T, axis=0, keepdims=True), (8, 128))
        scaled[k] = (block * gain_ref[...]).astype(BF16)
        for by in range(1, SIDE):
            q_copy(g, by).start()

        @pl.when(g != y)
        def _():
            q_copy(g, 0).start()

        @pl.when(g == y)
        def _():
            recv_q[ctx] = send_q[g]

    first = (x, y)
    second = (y, x)

    def partial(k, h, c):
        g = turn(z, offsets[k])
        part = parts[h][c]
        result = jnp.dot(
            scaled[k], weights[h][:, STARTS[c]:STARTS[c] + CHUNKS[c]],
            preferred_element_type=F32)
        for b in range(SIDE):
            if h == 0:
                part[b, g] = result[32 * b:32 * b + 32]
            else:
                part[g, b] = result[32 * b:32 * b + 32]

    def near(h, step, by):
        along_x = (h == 0) == (step == 0)
        return turn(x, by) + SIDE * y if along_x else x + SIDE * turn(y, by)

    last = n - 1

    def link(h, c, kind):
        if c == last and kind == 4:
            src, dst, by = t1_out[h][c], t0_in[h], 2
        else:
            src, dst, by = ends(h, c, kind)
        i = (h * n + c) * 8 + kind
        return pltpu.make_async_remote_copy(
            src_ref=src, dst_ref=dst, send_sem=r_send.at[i], recv_sem=r_recv.at[i],
            device_id={"ctx": near(h, 0 if kind < 4 else 1, by)}, device_id_type=MESH)

    def ends(h, c, kind):
        return (
            (s1_out[h][c].at[pl.ds(0, 2)], s1p_in[h][c], 1),
            (s1_out[h][c].at[pl.ds(2, 2)], s1m_in[h][c], 3),
            (s2p_out[h][c], s2p_in[h][c], 1),
            (s2m_out[h][c], s2m_in[h][c], 3),
            (t1_out[h][c].at[pl.ds(0, 16)], t1p_in[h][c], 1),
            (t1_out[h][c].at[pl.ds(16, 16)], t1m_in[h][c], 3),
            (t2p_out[h][c], t2p_in[h][c], 1),
            (t2m_out[h][c], t2m_in[h][c], 3),
        )[kind]

    top, bottom = pl.ds(0, 16), pl.ds(16, 16)

    def step1(h, c):
        s1_out[h][c][...] = parts[h][c][turn(first[h], 2)].astype(BF16)
        link(h, c, 0).start()
        link(h, c, 1).start()

    def step2(h, c):
        part, ahead, behind = parts[h][c], turn(first[h], 1), turn(first[h], 3)
        link(h, c, 0).wait_recv()
        for b in range(2):
            s2p_out[h][c][b] = (part[ahead, b] + s1p_in[h][c][b].astype(F32)).astype(BF16)
            s2p_out[h][c][2 + b] = part[ahead, 2 + b].astype(BF16)
        link(h, c, 2).start()
        link(h, c, 1).wait_recv()
        for b in range(2):
            s2m_out[h][c][b] = part[behind, b].astype(BF16)
            s2m_out[h][c][2 + b] = (
                part[behind, 2 + b] + s1m_in[h][c][b].astype(F32)).astype(BF16)
        link(h, c, 3).start()

    def step3(h, c):
        part, f, s = parts[h][c], first[h], second[h]
        link(h, c, 2).wait_recv()
        link(h, c, 3).wait_recv()
        for b in range(SIDE):
            part[f, b] = (
                part[f, b] + s2p_in[h][c][b].astype(F32) + s2m_in[h][c][b].astype(F32))
        t1_out[h][c][...] = part[f, turn(s, 2)].astype(BF16)
        link(h, c, 4).start()
        if c == last:
            t2p_out[h][c][...] = part[f, turn(s, 1)].astype(BF16)
            link(h, c, 6).start()
            t2m_out[h][c][...] = part[f, turn(s, 3)].astype(BF16)
            link(h, c, 7).start()
        else:
            link(h, c, 5).start()

    def step4(h, c):
        part, f, s = parts[h][c], first[h], second[h]
        ahead, behind = turn(s, 1), turn(s, 3)
        link(h, c, 4).wait_recv()
        t2p_out[h][c][top] = (part[f, ahead, top] + t1p_in[h][c][...].astype(F32)).astype(BF16)
        t2p_out[h][c][bottom] = part[f, ahead, bottom].astype(BF16)
        link(h, c, 6).start()
        link(h, c, 5).wait_recv()
        t2m_out[h][c][top] = part[f, behind, top].astype(BF16)
        t2m_out[h][c][bottom] = (
            part[f, behind, bottom] + t1m_in[h][c][...].astype(F32)).astype(BF16)
        link(h, c, 7).start()

    def finish(c, scale):
        at = slice(STARTS[c], STARTS[c] + CHUNKS[c])
        for h, out in enumerate((gate_ref, up_ref)):
            total = parts[h][c][first[h], second[h]]
            link(h, c, 6).wait_recv()
            total += t2p_in[h][c][...].astype(F32)
            link(h, c, 7).wait_recv()
            total += t2m_in[h][c][...].astype(F32)
            if c == last:
                link(h, c, 4).wait_recv()
                total += t0_in[h][...].astype(F32)
            out[:, at] = total * scale

    def multiply(k):
        for c in range(n):
            for h in range(2):
                partial(k, h, c)

    mate = 1 - core
    before, after, across = (turn(z, by) * 2 + mate for by in (3, 1, 2))
    loads["acts"].wait()
    z_copy(4, other, 0, other, whole=True).wait_recv()
    prepare(0)
    loads["wg"].wait()
    loads["wu"].wait()
    multiply(0)

    passed = []

    def forward(*copies):
        for copy in copies:
            copy.start()
            passed.append(copy)

    z_copy(0, left, 0, right).wait_recv()
    forward(z_copy(5, left, 0, right), z_copy(11, left, 0, right_mate))
    z_copy(1, right, 1, left).wait_recv()
    forward(z_copy(6, right, 1, left), z_copy(12, right, 1, left_mate))
    z_copy(2, left, 1, right).wait_recv()
    forward(z_copy(7, left, 0, other, whole=True))
    z_copy(3, right, 0, left).wait_recv()
    forward(z_copy(8, right, 0, other, whole=True))
    convolve()
    c_start()
    recv_c[ctx] = send_c[ctx]
    z_copy(7, before, 0, other, whole=True).wait_recv()
    prepare(1)
    multiply(1)
    z_copy(8, after, 0, other, whole=True).wait_recv()
    prepare(2)
    multiply(2)
    z_copy(5, far, 0, right).wait_recv()
    z_copy(6, far, 1, left).wait_recv()
    z_copy(11, across, 0, right_mate).wait_recv()
    z_copy(12, across, 1, left_mate).wait_recv()
    prepare(3)
    for c in range(n):
        for h in range(2):
            partial(3, h, c)
            step1(h, c)

    scale = None
    for c in range(n + 3):
        if c < n:
            step2(0, c)
            step2(1, c)
        if 0 <= c - 1 < n:
            step3(0, c - 1)
            step3(1, c - 1)
        if 0 <= c - 2 < last:
            step4(0, c - 2)
            step4(1, c - 2)
        if c == 0:
            for copy in own + passed:
                copy.wait_send()
            u_drain()
        if c == 1:
            c_wait()
            loads["query"].wait()
            direct_gain = skip_ref[...].astype(F32)
            for i in range(GROUP // 2):
                at = slice(128 * i, 128 * i + 128)
                even = recv_c[2 * i].astype(F32)
                odd = recv_c[2 * i + 1].astype(F32)
                conv = jnp.concatenate(
                    (jnp.where(low_half[:64], even, pltpu.roll(odd, 64, 1)),
                     jnp.where(low_half[:64], pltpu.roll(even, 64, 1), odd)), axis=0)
                direct = direct_gain[at].reshape(1, 128) * mixed[:, at].astype(F32)
                gated_ref[:, at] = (
                    query[:, at].astype(F32) * (conv + direct)).astype(BF16)
            c_drain()
        if c == 2:
            @pl.loop(1, GROUP)
            def _(i):
                peer = lax.rem(ctx + i, GROUP)
                pltpu.make_async_remote_copy(
                    src_ref=send_q.at[0], dst_ref=recv_q.at[peer],
                    send_sem=q_send.at[peer], recv_sem=q_recv.at[peer],
                    device_id={"ctx": peer}, device_id_type=MESH).wait_recv()

            power = recv_q[0]
            for i in range(1, GROUP):
                power = power + recv_q[i]
            spread[...] = jnp.broadcast_to(power[0:1], (128, 128)).T
            mine = spread[pl.ds(pl.multiple_of(32 * x, 32), 32), :]
            scale = lax.rsqrt(mine[:, :1] / D + EPSILON)
            for k in range(SIDE):
                g = turn(z, offsets[k])
                for by in range(1, SIDE):
                    q_copy(g, by).wait_send()

                @pl.when(g != y)
                def _(g=g):
                    q_copy(g, 0).wait_send()
        if c >= 3:
            finish(c - 3, scale)
            for h in range(2):
                for kind in range(8):
                    if c - 3 != last or kind != 5:
                        link(h, c - 3, kind).wait_send()


def body(query_b, key_b, value_b, filter_b, skip_b, acts_a, gain_a, w_gate, w_up, grad_hidden):
    high, low, back = dft_tables()
    any_spec = pl.BlockSpec(memory_space=pl.ANY)
    vmem = pl.BlockSpec(memory_space=pltpu.VMEM)
    length, width = key_b.shape
    hidden = w_gate.shape[1]

    def per_chunk(*lead, kind=BF16):
        return [pltpu.VMEM(lead + (w,), kind) for w in CHUNKS] * 2

    scratch = [
        pltpu.VMEM((length, width), BF16),
        pltpu.VMEM((length, width), BF16),
        pltpu.VMEM((length, width), BF16),
        pltpu.VMEM((length, width), BF16),
        pltpu.VMEM(w_gate.shape, BF16),
        pltpu.VMEM(w_up.shape, BF16),
        pltpu.VMEM(high.shape, BF16),
        pltpu.VMEM(low.shape, BF16),
        pltpu.VMEM(back.shape, BF16),
        pltpu.VMEM((length, width), BF16),
        pltpu.VMEM((GROUP, 128, 128), BF16),
        pltpu.VMEM((GROUP, 128, 128), BF16),
        pltpu.VMEM((8, 2 * BLOCK, 128), F32),
        pltpu.VMEM((8, 2 * BLOCK, 128), F32),
        pltpu.VMEM((8, 2 * BLOCK, 128), BF16),
        pltpu.VMEM((GROUP, 64, 128), BF16),
        pltpu.VMEM((GROUP, 64, 128), BF16),
        pltpu.VMEM((8, 64, 512), BF16),
        pltpu.VMEM((SIDE, 128, 512), BF16),
        pltpu.VMEM((SIDE, 8, 128), F32),
        pltpu.VMEM((GROUP, 8, 128), F32),
        pltpu.VMEM((128, 128), F32),
    ]
    scratch += per_chunk(SIDE, SIDE, 32, kind=F32)
    for lead in (
        (SIDE, 32), (2, 32), (2, 32), (SIDE, 32), (SIDE, 32), (SIDE, 32), (SIDE, 32),
        (32,), (16,), (16,), (32,), (32,), (32,), (32,),
    ):
        scratch += per_chunk(*lead)
    scratch += [pltpu.VMEM((32, CHUNKS[-1]), BF16)] * 2
    links = 2 * len(CHUNKS) * 8
    for size in (10, GROUP, GROUP, GROUP, GROUP, GROUP, GROUP, 13, 13, links, links):
        scratch.append(pltpu.SemaphoreType.DMA((size,)))
    gated, gate, up = pl.pallas_call(
        kernel,
        out_shape=(
            pltpu.VMEM((length, width), BF16),
            pltpu.VMEM(grad_hidden.shape, F32),
            pltpu.VMEM(grad_hidden.shape, F32),
        ),
        in_specs=[any_spec] * 4 + [vmem, any_spec, vmem] + [any_spec] * 5,
        out_specs=(vmem, vmem, vmem),
        scratch_shapes=scratch,
        compiler_params=pltpu.CompilerParams(
            collective_id=0, has_side_effects=True, vmem_limit_bytes=56 * 1024 * 1024),
        name="hyena",
    )(
        query_b, key_b, value_b, filter_b, skip_b, acts_a,
        gain_a.reshape(1, -1), w_gate, w_up,
        jnp.asarray(high), jnp.asarray(low), jnp.asarray(back),
    )
    sigma = jax.nn.sigmoid(gate)
    upstream = grad_hidden.astype(F32)
    grad_gate = (upstream * up * sigma * (1.0 + gate * (1.0 - sigma))).astype(BF16)
    grad_up = (upstream * gate * sigma).astype(BF16)
    return gated, grad_gate, grad_up


def solution(mesh):
    return jax.shard_map(
        body,
        mesh=mesh,
        in_specs=(
            P(("dp", "ctx"), "tp"),
            P(("dp", "ctx"), "tp"),
            P(("dp", "ctx"), "tp"),
            P("ctx", "tp"),
            P("tp"),
            P(("dp", "tp"), "ctx"),
            P("ctx"),
            P("ctx", "tp"),
            P("ctx", "tp"),
            P(("dp", "ctx"), "tp"),
        ),
        out_specs=(P(("dp", "ctx"), "tp"), P(("dp", "ctx"), "tp"), P(("dp", "ctx"), "tp")),
        check_vma=False,
    )
```

```python
import math

import jax
import jax.numpy as jnp
import numpy as np
from jax import lax
from jax.experimental import pallas as pl
from jax.experimental.pallas import tpu as pltpu
from jax.sharding import PartitionSpec as P

D = 8192
EPSILON = 1e-06
SIDE = 4
GROUP = 16
BLOCK = 256
CHUNKS = (768, 640)
STARTS = tuple(sum(CHUNKS[:i]) for i in range(len(CHUNKS)))
MESH = pl.DeviceIdType.MESH
F32 = jnp.float32
BF16 = jnp.bfloat16


def dft_tables():
    order = np.concatenate((np.arange(0, BLOCK, 2), np.arange(1, BLOCK, 2)))
    angle = np.outer(2 * order + 1, np.arange(BLOCK)) % (4 * BLOCK)
    angle = angle.astype(np.float64) * (math.pi / (2 * BLOCK))
    full = np.concatenate((np.cos(angle), -np.sin(angle)), axis=0)
    high = full.astype(jnp.bfloat16)
    low = (full - high.astype(np.float64)).astype(jnp.bfloat16)
    back = np.ascontiguousarray((full.T / BLOCK)).astype(jnp.bfloat16)
    return high, low, back


def kernel(
    query_h, key_h, value_h, taps_h, skip_ref, acts_h, gain_ref, wg_h, wu_h,
    high_h, low_h, back_h,
    gated_ref, gate_ref, up_ref,
    query, key, value, taps, wg, wu, high, low, back,
    mixed, send_u, recv_u, spec, turned, joint, send_c, recv_c,
    rows, scaled, send_q, recv_q, spread,
    *rest,
):
    n = len(CHUNKS)
    (parts, s1_out, s1p_in, s1m_in, s2p_out, s2m_out, s2p_in, s2m_in,
     t1_out, t1p_in, t1m_in, t2p_out, t2m_out, t2p_in, t2m_in) = (
        (rest[2 * i * n:(2 * i + 1) * n], rest[(2 * i + 1) * n:(2 * i + 2) * n])
        for i in range(15)
    )
    t0_in = (rest[30 * n:31 * n], rest[31 * n:32 * n])
    (load_sem, u_send, u_recv, c_send, c_recv, q_send, q_recv, z_send, z_recv,
     r_send, r_recv) = rest[32 * n:]

    ctx = lax.axis_index("ctx")
    tp = lax.axis_index("tp")
    y, x = lax.div(ctx, SIDE), lax.rem(ctx, SIDE)
    z, core = lax.div(tp, 2), lax.rem(tp, 2)

    def turn(value_, by):
        return lax.rem(value_ + by, SIDE)

    left = turn(z, 3) * 2 + core
    right = turn(z, 1) * 2 + core
    far = turn(z, 2) * 2 + core
    other = z * 2 + 1 - core
    left_mate, right_mate = turn(z, 3) * 2 + 1 - core, turn(z, 1) * 2 + 1 - core

    barrier = pltpu.get_barrier_semaphore()

    @pl.loop(1, GROUP)
    def _(k):
        pl.semaphore_signal(
            barrier, inc=1, device_id={"ctx": lax.rem(ctx + k, GROUP)}, device_id_type=MESH)

    for peer in (left, right, other, left_mate, right_mate):
        pl.semaphore_signal(barrier, inc=1, device_id={"tp": peer}, device_id_type=MESH)

    loads = {}
    for i, (name, src, dst) in enumerate((
        ("key", key_h, key), ("value", value_h, value), ("taps", taps_h, taps),
        ("acts", acts_h, rows.at[tp]), ("high", high_h, high), ("low", low_h, low),
        ("wg", wg_h, wg), ("wu", wu_h, wu), ("back", back_h, back),
        ("query", query_h, query),
    )):
        loads[name] = pltpu.make_async_copy(src, dst, load_sem.at[i])
        loads[name].start()

    lane = lax.broadcasted_iota(jnp.int32, (128, 128), 1)
    low_half = lane < 64

    pl.semaphore_wait(barrier, GROUP + 4)

    def z_copy(i, block, half, peer, whole=False, first=False):
        part = pl.ds(0, 64) if whole else pl.ds(32 * half, 32)
        at = rows.at[block, part]
        return pltpu.make_async_remote_copy(
            src_ref=acts_h.at[part] if first else at, dst_ref=at,
            send_sem=z_send.at[i], recv_sem=z_recv.at[i],
            device_id={"tp": peer}, device_id_type=MESH)

    own = [
        z_copy(0, tp, 0, right, first=True), z_copy(1, tp, 1, left, first=True),
        z_copy(4, tp, 0, other, whole=True, first=True),
        z_copy(2, tp, 1, right, first=True), z_copy(3, tp, 0, left, first=True),
    ]
    for copy in own[:3]:
        copy.start()

    for name in ("key", "value", "taps"):
        loads[name].wait()

    @pl.loop(0, GROUP // 2)
    def _(i):
        at = pl.ds(pl.multiple_of(i * 128, 128), 128)
        signal = (key[:, at].astype(F32) * value[:, at].astype(F32)).astype(BF16)
        mixed[:, at] = signal
        signal = signal.astype(F32)
        lags = taps[:, at].astype(F32)
        send_u[2 * i] = jnp.where(low_half, signal, pltpu.roll(lags, 64, 1)).astype(BF16)
        send_u[2 * i + 1] = jnp.where(low_half, pltpu.roll(signal, 64, 1), lags).astype(BF16)


    def exchange(src, dst, send_sem, recv_sem):
        def one(k):
            peer = lax.rem(ctx + k, GROUP)
            return pltpu.make_async_remote_copy(
                src_ref=src.at[peer], dst_ref=dst.at[ctx],
                send_sem=send_sem.at[peer], recv_sem=recv_sem.at[ctx],
                device_id={"ctx": peer}, device_id_type=MESH)

        def arrival(k):
            peer = lax.rem(ctx + k, GROUP)
            return pltpu.make_async_remote_copy(
                src_ref=src.at[peer], dst_ref=dst.at[peer],
                send_sem=send_sem.at[peer], recv_sem=recv_sem.at[peer],
                device_id={"ctx": peer}, device_id_type=MESH)

        def start():
            @pl.loop(1, GROUP)
            def _(k):
                one(k).start()

        def wait_recv():
            @pl.loop(1, GROUP)
            def _(k):
                arrival(k).wait_recv()

        def wait_send():
            @pl.loop(1, GROUP)
            def _(k):
                one(k).wait_send()

        return start, wait_recv, wait_send

    u_start, u_wait, u_drain = exchange(send_u, recv_u, u_send, u_recv)
    c_start, c_wait, c_drain = exchange(send_c, recv_c, c_send, c_recv)
    u_start()
    recv_u[ctx] = send_u[ctx]
    for copy in own[3:]:
        copy.start()

    def convolve():
        u_wait()
        loads["high"].wait()
        loads["low"].wait()

        @pl.loop(0, 4)
        def _(i):
            pair = jnp.concatenate(
                (recv_u[pl.ds(4 * i, 2)].reshape(BLOCK, 128),
                 recv_u[pl.ds(4 * i + 2, 2)].reshape(BLOCK, 128)), axis=1)
            result = jnp.dot(high[...], pair, preferred_element_type=F32)
            result += jnp.dot(low[...], pair, preferred_element_type=F32)
            for h in range(2):
                half = result[:, 128 * h:128 * h + 128]
                spec[2 * i + h] = half
                turned[2 * i + h] = pltpu.roll(half, 64, 1)

        @pl.loop(0, 16)
        def _(r):
            re = pl.ds(pl.multiple_of(16 * r, 16), 16)
            im = pl.ds(pl.multiple_of(BLOCK + 16 * r, 16), 16)
            sign = 1.0 - 2.0 * lax.div(r, 8).astype(F32)
            last = None
            for i in range(8):
                total_re = total_im = None
                for a in range(i // 2 + 1):
                    b = i - a
                    a_re, a_im = spec[a, re], spec[a, im]
                    b_re, b_im = turned[b, re], turned[b, im]
                    one_re = a_re * b_re - a_im * b_im
                    one_im = a_re * b_im + a_im * b_re
                    if a == b:
                        one_re, one_im = 0.5 * one_re, 0.5 * one_im
                    total_re = one_re if total_re is None else total_re + one_re
                    total_im = one_im if total_im is None else total_im + one_im
                if last is None:
                    joint[i, re] = total_re.astype(BF16)
                    joint[i, im] = total_im.astype(BF16)
                else:
                    joint[i, re] = (total_re - sign * last[1]).astype(BF16)
                    joint[i, im] = (total_im + sign * last[0]).astype(BF16)
                last = (total_re, total_im)

        loads["back"].wait()

        @pl.loop(0, 4)
        def _(i):
            pair = jnp.concatenate((joint[2 * i], joint[2 * i + 1]), axis=1)
            result = jnp.dot(back[...], pair, preferred_element_type=F32)
            for h in range(2):
                half = result[:, 128 * h:128 * h + 128]
                half = half + pltpu.roll(half, 64, 1)
                for d in range(2):
                    send_c[4 * i + 2 * h + d] = jnp.where(
                        low_half[:64], half[128 * d:128 * d + 64], half[128 * d + 64:128 * d + 128]
                    ).astype(BF16)


    weights = (wg, wu)
    offsets = (0, 3, 1, 2)

    def q_copy(g, by):
        peer = SIDE * g + turn(x, by)
        return pltpu.make_async_remote_copy(
            src_ref=send_q.at[g], dst_ref=recv_q.at[ctx],
            send_sem=q_send.at[peer], recv_sem=q_recv.at[ctx],
            device_id={"ctx": peer}, device_id_type=MESH)

    def prepare(k):
        g = turn(z, offsets[k])
        block = rows[pl.ds(2 * g, 2)].reshape(128, 512).astype(F32)
        scaled[k] = (block * gain_ref[...]).astype(BF16)

    def squares_of(k):
        g = turn(z, offsets[k])
        block = rows[pl.ds(2 * g, 2)].reshape(128, 512).astype(F32)
        squares = block * block
        squares = (squares[:, :128] + squares[:, 128:256]) + (
            squares[:, 256:384] + squares[:, 384:])
        send_q[g] = jnp.broadcast_to(jnp.sum(squares.T, axis=0, keepdims=True), (8, 128))
        for by in range(1, SIDE):
            q_copy(g, by).start()

        @pl.when(g != y)
        def _():
            q_copy(g, 0).start()

        @pl.when(g == y)
        def _():
            recv_q[ctx] = send_q[g]

    first = (x, y)
    second = (y, x)

    def partial(k, h, c):
        g = turn(z, offsets[k])
        part = parts[h][c]
        result = jnp.dot(
            scaled[k], weights[h][:, STARTS[c]:STARTS[c] + CHUNKS[c]],
            preferred_element_type=F32)
        for b in range(SIDE):
            if h == 0:
                part[b, g] = result[32 * b:32 * b + 32]
            else:
                part[g, b] = result[32 * b:32 * b + 32]

    def near(h, step, by):
        along_x = (h == 0) == (step == 0)
        return turn(x, by) + SIDE * y if along_x else x + SIDE * turn(y, by)

    last = n - 1

    def link(h, c, kind):
        if kind == 4:
            src, dst, by = t1_out[h][c], t0_in[h][c], 2
        else:
            src, dst, by = ends(h, c, kind)
        i = (h * n + c) * 8 + kind
        return pltpu.make_async_remote_copy(
            src_ref=src, dst_ref=dst, send_sem=r_send.at[i], recv_sem=r_recv.at[i],
            device_id={"ctx": near(h, 0 if kind < 4 else 1, by)}, device_id_type=MESH)

    def ends(h, c, kind):
        return (
            (s1_out[h][c].at[pl.ds(0, 2)], s1p_in[h][c], 1),
            (s1_out[h][c].at[pl.ds(2, 2)], s1m_in[h][c], 3),
            (s2p_out[h][c], s2p_in[h][c], 1),
            (s2m_out[h][c], s2m_in[h][c], 3),
            (t1_out[h][c].at[pl.ds(0, 16)], t1p_in[h][c], 1),
            (t1_out[h][c].at[pl.ds(16, 16)], t1m_in[h][c], 3),
            (t2p_out[h][c], t2p_in[h][c], 1),
            (t2m_out[h][c], t2m_in[h][c], 3),
        )[kind]

    top, bottom = pl.ds(0, 16), pl.ds(16, 16)

    def step1(h, c):
        s1_out[h][c][...] = parts[h][c][turn(first[h], 2)].astype(BF16)
        link(h, c, 0).start()
        link(h, c, 1).start()

    def step2(h, c):
        part, ahead, behind = parts[h][c], turn(first[h], 1), turn(first[h], 3)
        link(h, c, 0).wait_recv()
        for b in range(2):
            s2p_out[h][c][b] = (part[ahead, b] + s1p_in[h][c][b].astype(F32)).astype(BF16)
            s2p_out[h][c][2 + b] = part[ahead, 2 + b].astype(BF16)
        link(h, c, 2).start()
        link(h, c, 1).wait_recv()
        for b in range(2):
            s2m_out[h][c][b] = part[behind, b].astype(BF16)
            s2m_out[h][c][2 + b] = (
                part[behind, 2 + b] + s1m_in[h][c][b].astype(F32)).astype(BF16)
        link(h, c, 3).start()

    def step3(h, c):
        part, f, s = parts[h][c], first[h], second[h]
        link(h, c, 2).wait_recv()
        link(h, c, 3).wait_recv()
        for b in range(SIDE):
            part[f, b] = (
                part[f, b] + s2p_in[h][c][b].astype(F32) + s2m_in[h][c][b].astype(F32))
        t1_out[h][c][...] = part[f, turn(s, 2)].astype(BF16)
        link(h, c, 4).start()
        t2p_out[h][c][...] = part[f, turn(s, 1)].astype(BF16)
        link(h, c, 6).start()
        t2m_out[h][c][...] = part[f, turn(s, 3)].astype(BF16)
        link(h, c, 7).start()

    def step4(h, c):
        part, f, s = parts[h][c], first[h], second[h]
        ahead, behind = turn(s, 1), turn(s, 3)
        link(h, c, 4).wait_recv()
        t2p_out[h][c][top] = (part[f, ahead, top] + t1p_in[h][c][...].astype(F32)).astype(BF16)
        t2p_out[h][c][bottom] = part[f, ahead, bottom].astype(BF16)
        link(h, c, 6).start()
        link(h, c, 5).wait_recv()
        t2m_out[h][c][top] = part[f, behind, top].astype(BF16)
        t2m_out[h][c][bottom] = (
            part[f, behind, bottom] + t1m_in[h][c][...].astype(F32)).astype(BF16)
        link(h, c, 7).start()

    def finish(c, scale):
        at = slice(STARTS[c], STARTS[c] + CHUNKS[c])
        for h, out in enumerate((gate_ref, up_ref)):
            total = parts[h][c][first[h], second[h]]
            link(h, c, 6).wait_recv()
            total += t2p_in[h][c][...].astype(F32)
            link(h, c, 7).wait_recv()
            total += t2m_in[h][c][...].astype(F32)
            if True:
                link(h, c, 4).wait_recv()
                total += t0_in[h][c][...].astype(F32)
            out[:, at] = total * scale

    def multiply(k):
        for c in range(n):
            for h in range(2):
                partial(k, h, c)

    mate = 1 - core
    before, after, across = (turn(z, by) * 2 + mate for by in (3, 1, 2))
    loads["acts"].wait()
    z_copy(4, other, 0, other, whole=True).wait_recv()
    prepare(0)
    squares_of(0)
    loads["wg"].wait()
    loads["wu"].wait()
    multiply(0)

    passed = []

    def forward(*copies):
        for copy in copies:
            copy.start()
            passed.append(copy)

    z_copy(0, left, 0, right).wait_recv()
    forward(z_copy(5, left, 0, right), z_copy(11, left, 0, right_mate))
    z_copy(1, right, 1, left).wait_recv()
    forward(z_copy(6, right, 1, left), z_copy(12, right, 1, left_mate))
    z_copy(2, left, 1, right).wait_recv()
    forward(z_copy(7, left, 0, other, whole=True))
    z_copy(3, right, 0, left).wait_recv()
    forward(z_copy(8, right, 0, other, whole=True))
    convolve()
    c_start()
    recv_c[ctx] = send_c[ctx]
    z_copy(7, before, 0, other, whole=True).wait_recv()
    prepare(1)
    squares_of(1)
    multiply(1)
    z_copy(8, after, 0, other, whole=True).wait_recv()
    prepare(2)
    squares_of(2)
    multiply(2)

    @pl.when(y != z)
    def _():
        for c in range(n):
            step1(1, c)

    z_copy(5, far, 0, right).wait_recv()
    z_copy(6, far, 1, left).wait_recv()
    z_copy(11, across, 0, right_mate).wait_recv()
    z_copy(12, across, 1, left_mate).wait_recv()
    prepare(3)
    for c in range(n):
        partial(3, 0, c)
        step1(0, c)
        partial(3, 1, c)

        @pl.when(y == z)
        def _(c=c):
            step1(1, c)

    squares_of(3)

    scale = None
    for c in range(n + 2):
        if c < n:
            step2(0, c)
            step2(1, c)
        if 0 <= c - 1 < n:
            step3(0, c - 1)
            step3(1, c - 1)
        if False:
            step4(0, c - 2)
            step4(1, c - 2)
        if c == 0:
            for copy in own + passed:
                copy.wait_send()
            u_drain()
        if c == 1:
            c_wait()
            loads["query"].wait()
            direct_gain = skip_ref[...].astype(F32)
            for i in range(GROUP // 2):
                at = slice(128 * i, 128 * i + 128)
                even = recv_c[2 * i].astype(F32)
                odd = recv_c[2 * i + 1].astype(F32)
                conv = jnp.concatenate(
                    (jnp.where(low_half[:64], even, pltpu.roll(odd, 64, 1)),
                     jnp.where(low_half[:64], pltpu.roll(even, 64, 1), odd)), axis=0)
                direct = direct_gain[at].reshape(1, 128) * mixed[:, at].astype(F32)
                gated_ref[:, at] = (
                    query[:, at].astype(F32) * (conv + direct)).astype(BF16)
            c_drain()
        if c == 2:
            @pl.loop(1, GROUP)
            def _(i):
                peer = lax.rem(ctx + i, GROUP)
                pltpu.make_async_remote_copy(
                    src_ref=send_q.at[0], dst_ref=recv_q.at[peer],
                    send_sem=q_send.at[peer], recv_sem=q_recv.at[peer],
                    device_id={"ctx": peer}, device_id_type=MESH).wait_recv()

            power = recv_q[0]
            for i in range(1, GROUP):
                power = power + recv_q[i]
            spread[...] = jnp.broadcast_to(power[0:1], (128, 128)).T
            mine = spread[pl.ds(pl.multiple_of(32 * x, 32), 32), :]
            scale = lax.rsqrt(mine[:, :1] / D + EPSILON)
            for k in range(SIDE):
                g = turn(z, offsets[k])
                for by in range(1, SIDE):
                    q_copy(g, by).wait_send()

                @pl.when(g != y)
                def _(g=g):
                    q_copy(g, 0).wait_send()
        if c >= 2:
            finish(c - 2, scale)
            for h in range(2):
                for kind in range(8):
                    if kind != 5:
                        link(h, c - 2, kind).wait_send()


def body(query_b, key_b, value_b, filter_b, skip_b, acts_a, gain_a, w_gate, w_up, grad_hidden):
    high, low, back = dft_tables()
    any_spec = pl.BlockSpec(memory_space=pl.ANY)
    vmem = pl.BlockSpec(memory_space=pltpu.VMEM)
    length, width = key_b.shape
    hidden = w_gate.shape[1]

    def per_chunk(*lead, kind=BF16):
        return [pltpu.VMEM(lead + (w,), kind) for w in CHUNKS] * 2

    scratch = [
        pltpu.VMEM((length, width), BF16),
        pltpu.VMEM((length, width), BF16),
        pltpu.VMEM((length, width), BF16),
        pltpu.VMEM((length, width), BF16),
        pltpu.VMEM(w_gate.shape, BF16),
        pltpu.VMEM(w_up.shape, BF16),
        pltpu.VMEM(high.shape, BF16),
        pltpu.VMEM(low.shape, BF16),
        pltpu.VMEM(back.shape, BF16),
        pltpu.VMEM((length, width), BF16),
        pltpu.VMEM((GROUP, 128, 128), BF16),
        pltpu.VMEM((GROUP, 128, 128), BF16),
        pltpu.VMEM((8, 2 * BLOCK, 128), F32),
        pltpu.VMEM((8, 2 * BLOCK, 128), F32),
        pltpu.VMEM((8, 2 * BLOCK, 128), BF16),
        pltpu.VMEM((GROUP, 64, 128), BF16),
        pltpu.VMEM((GROUP, 64, 128), BF16),
        pltpu.VMEM((8, 64, 512), BF16),
        pltpu.VMEM((SIDE, 128, 512), BF16),
        pltpu.VMEM((SIDE, 8, 128), F32),
        pltpu.VMEM((GROUP, 8, 128), F32),
        pltpu.VMEM((128, 128), F32),
    ]
    scratch += per_chunk(SIDE, SIDE, 32, kind=F32)
    for lead in (
        (SIDE, 32), (2, 32), (2, 32), (SIDE, 32), (SIDE, 32), (SIDE, 32), (SIDE, 32),
        (32,), (16,), (16,), (32,), (32,), (32,), (32,),
    ):
        scratch += per_chunk(*lead)
    scratch += per_chunk(32)
    links = 2 * len(CHUNKS) * 8
    for size in (10, GROUP, GROUP, GROUP, GROUP, GROUP, GROUP, 13, 13, links, links):
        scratch.append(pltpu.SemaphoreType.DMA((size,)))
    gated, gate, up = pl.pallas_call(
        kernel,
        out_shape=(
            pltpu.VMEM((length, width), BF16),
            pltpu.VMEM(grad_hidden.shape, F32),
            pltpu.VMEM(grad_hidden.shape, F32),
        ),
        in_specs=[any_spec] * 4 + [vmem, any_spec, vmem] + [any_spec] * 5,
        out_specs=(vmem, vmem, vmem),
        scratch_shapes=scratch,
        compiler_params=pltpu.CompilerParams(
            collective_id=0, has_side_effects=True, vmem_limit_bytes=56 * 1024 * 1024),
        name="hyena",
    )(
        query_b, key_b, value_b, filter_b, skip_b, acts_a,
        gain_a.reshape(1, -1), w_gate, w_up,
        jnp.asarray(high), jnp.asarray(low), jnp.asarray(back),
    )
    sigma = jax.nn.sigmoid(gate)
    upstream = grad_hidden.astype(F32)
    grad_gate = (upstream * up * sigma * (1.0 + gate * (1.0 - sigma))).astype(BF16)
    grad_up = (upstream * gate * sigma).astype(BF16)
    return gated, grad_gate, grad_up


def solution(mesh):
    return jax.shard_map(
        body,
        mesh=mesh,
        in_specs=(
            P(("dp", "ctx"), "tp"),
            P(("dp", "ctx"), "tp"),
            P(("dp", "ctx"), "tp"),
            P("ctx", "tp"),
            P("tp"),
            P(("dp", "tp"), "ctx"),
            P("ctx"),
            P("ctx", "tp"),
            P("ctx", "tp"),
            P(("dp", "ctx"), "tp"),
        ),
        out_specs=(P(("dp", "ctx"), "tp"), P(("dp", "ctx"), "tp"), P(("dp", "ctx"), "tp")),
        check_vma=False,
    )
```

```python
import math

import jax
import jax.numpy as jnp
from jax import lax
from jax.experimental import pallas as pl
from jax.experimental.pallas import tpu as pltpu
from jax.sharding import PartitionSpec as P

D = 8192
EPSILON = 1e-06
SIDE = 4
GROUP = 16
BLOCK = 256
CHUNKS = (768, 640)
STARTS = tuple(sum(CHUNKS[:i]) for i in range(len(CHUNKS)))
MESH = pl.DeviceIdType.MESH
F32 = jnp.float32
BF16 = jnp.bfloat16


def fill_tables(high, low, back):
    half = BLOCK // 2

    @pl.loop(0, BLOCK // 16)
    def _(i):
        row = lax.broadcasted_iota(jnp.int32, (16, BLOCK), 0) + 16 * i
        order = 2 * row - jnp.where(row >= half, BLOCK - 1, 0)
        turns = (2 * order + 1) * lax.broadcasted_iota(jnp.int32, (16, BLOCK), 1)
        turns = lax.rem(turns, 4 * BLOCK)
        turns = jnp.where(turns > 2 * BLOCK, turns - 4 * BLOCK, turns)
        angle = turns.astype(F32) * (math.pi / (2 * BLOCK))
        for start, value in ((0, jnp.cos(angle)), (BLOCK, -jnp.sin(angle))):
            at = pl.ds(pl.multiple_of(start + 16 * i, 16), 16)
            rounded = value.astype(BF16)
            high[at] = rounded
            low[at] = (value - rounded.astype(F32)).astype(BF16)

    back[...] = (high[...].astype(F32).T * (1.0 / BLOCK)).astype(BF16)


def kernel(
    query_h, key_h, value_h, taps_h, skip_ref, acts_h, gain_ref, wg_h, wu_h,
    gated_ref, gate_ref, up_ref,
    query, key, value, taps, wg, wu, high, low, back,
    mixed, send_u, recv_u, spec, turned, joint, send_c, recv_c,
    rows, scaled, send_q, recv_q, spread,
    *rest,
):
    n = len(CHUNKS)
    (parts, s1_out, s1p_in, s1m_in, s2p_out, s2m_out, s2p_in, s2m_in,
     t1_out, t1p_in, t1m_in, t2p_out, t2m_out, t2p_in, t2m_in) = (
        (rest[2 * i * n:(2 * i + 1) * n], rest[(2 * i + 1) * n:(2 * i + 2) * n])
        for i in range(15)
    )
    t0_in = (rest[30 * n:31 * n], rest[31 * n:32 * n])
    (load_sem, u_send, u_recv, c_send, c_recv, q_send, q_recv, z_send, z_recv,
     r_send, r_recv) = rest[32 * n:]

    ctx = lax.axis_index("ctx")
    tp = lax.axis_index("tp")
    y, x = lax.div(ctx, SIDE), lax.rem(ctx, SIDE)
    z, core = lax.div(tp, 2), lax.rem(tp, 2)

    def turn(value_, by):
        return lax.rem(value_ + by, SIDE)

    left = turn(z, 3) * 2 + core
    right = turn(z, 1) * 2 + core
    far = turn(z, 2) * 2 + core
    other = z * 2 + 1 - core
    left_mate, right_mate = turn(z, 3) * 2 + 1 - core, turn(z, 1) * 2 + 1 - core

    barrier = pltpu.get_barrier_semaphore()

    @pl.loop(1, GROUP)
    def _(k):
        pl.semaphore_signal(
            barrier, inc=1, device_id={"ctx": lax.rem(ctx + k, GROUP)}, device_id_type=MESH)

    for peer in (left, right, other, left_mate, right_mate):
        pl.semaphore_signal(barrier, inc=1, device_id={"tp": peer}, device_id_type=MESH)

    loads = {}
    for i, (name, src, dst) in enumerate((
        ("key", key_h, key), ("value", value_h, value), ("taps", taps_h, taps),
        ("acts", acts_h, rows.at[tp]),
        ("wg", wg_h, wg), ("wu", wu_h, wu),
        ("query", query_h, query),
    )):
        loads[name] = pltpu.make_async_copy(src, dst, load_sem.at[i])
        loads[name].start()

    lane = lax.broadcasted_iota(jnp.int32, (128, 128), 1)
    low_half = lane < 64

    pl.semaphore_wait(barrier, GROUP + 4)

    def z_copy(i, block, half, peer, whole=False, first=False):
        part = pl.ds(0, 64) if whole else pl.ds(32 * half, 32)
        at = rows.at[block, part]
        return pltpu.make_async_remote_copy(
            src_ref=acts_h.at[part] if first else at, dst_ref=at,
            send_sem=z_send.at[i], recv_sem=z_recv.at[i],
            device_id={"tp": peer}, device_id_type=MESH)

    own = [
        z_copy(0, tp, 0, right, first=True), z_copy(1, tp, 1, left, first=True),
        z_copy(4, tp, 0, other, whole=True, first=True),
        z_copy(2, tp, 1, right, first=True), z_copy(3, tp, 0, left, first=True),
    ]
    for copy in own[:3]:
        copy.start()

    for name in ("key", "value", "taps"):
        loads[name].wait()

    @pl.loop(0, GROUP // 2)
    def _(i):
        at = pl.ds(pl.multiple_of(i * 128, 128), 128)
        signal = (key[:, at].astype(F32) * value[:, at].astype(F32)).astype(BF16)
        mixed[:, at] = signal
        signal = signal.astype(F32)
        lags = taps[:, at].astype(F32)
        send_u[2 * i] = jnp.where(low_half, signal, pltpu.roll(lags, 64, 1)).astype(BF16)
        send_u[2 * i + 1] = jnp.where(low_half, pltpu.roll(signal, 64, 1), lags).astype(BF16)


    def exchange(src, dst, send_sem, recv_sem):
        def one(k):
            peer = lax.rem(ctx + k, GROUP)
            return pltpu.make_async_remote_copy(
                src_ref=src.at[peer], dst_ref=dst.at[ctx],
                send_sem=send_sem.at[peer], recv_sem=recv_sem.at[ctx],
                device_id={"ctx": peer}, device_id_type=MESH)

        def arrival(k):
            peer = lax.rem(ctx + k, GROUP)
            return pltpu.make_async_remote_copy(
                src_ref=src.at[peer], dst_ref=dst.at[peer],
                send_sem=send_sem.at[peer], recv_sem=recv_sem.at[peer],
                device_id={"ctx": peer}, device_id_type=MESH)

        def start():
            @pl.loop(1, GROUP)
            def _(k):
                one(k).start()

        def wait_recv():
            @pl.loop(1, GROUP)
            def _(k):
                arrival(k).wait_recv()

        def wait_send():
            @pl.loop(1, GROUP)
            def _(k):
                one(k).wait_send()

        return start, wait_recv, wait_send

    u_start, u_wait, u_drain = exchange(send_u, recv_u, u_send, u_recv)
    c_start, c_wait, c_drain = exchange(send_c, recv_c, c_send, c_recv)
    u_start()
    recv_u[ctx] = send_u[ctx]
    for copy in own[3:]:
        copy.start()

    def convolve():
        u_wait()

        @pl.loop(0, 4)
        def _(i):
            pair = jnp.concatenate(
                (recv_u[pl.ds(4 * i, 2)].reshape(BLOCK, 128),
                 recv_u[pl.ds(4 * i + 2, 2)].reshape(BLOCK, 128)), axis=1)
            result = jnp.dot(high[...], pair, preferred_element_type=F32)
            result += jnp.dot(low[...], pair, preferred_element_type=F32)
            for h in range(2):
                half = result[:, 128 * h:128 * h + 128]
                spec[2 * i + h] = half
                turned[2 * i + h] = pltpu.roll(half, 64, 1)

        @pl.loop(0, 16)
        def _(r):
            re = pl.ds(pl.multiple_of(16 * r, 16), 16)
            im = pl.ds(pl.multiple_of(BLOCK + 16 * r, 16), 16)
            sign = 1.0 - 2.0 * lax.div(r, 8).astype(F32)
            last = None
            for i in range(8):
                total_re = total_im = None
                for a in range(i // 2 + 1):
                    b = i - a
                    a_re, a_im = spec[a, re], spec[a, im]
                    b_re, b_im = turned[b, re], turned[b, im]
                    one_re = a_re * b_re - a_im * b_im
                    one_im = a_re * b_im + a_im * b_re
                    if a == b:
                        one_re, one_im = 0.5 * one_re, 0.5 * one_im
                    total_re = one_re if total_re is None else total_re + one_re
                    total_im = one_im if total_im is None else total_im + one_im
                if last is None:
                    joint[i, re] = total_re.astype(BF16)
                    joint[i, im] = total_im.astype(BF16)
                else:
                    joint[i, re] = (total_re - sign * last[1]).astype(BF16)
                    joint[i, im] = (total_im + sign * last[0]).astype(BF16)
                last = (total_re, total_im)


        @pl.loop(0, 4)
        def _(i):
            pair = jnp.concatenate((joint[2 * i], joint[2 * i + 1]), axis=1)
            result = jnp.dot(back[...], pair, preferred_element_type=F32)
            for h in range(2):
                half = result[:, 128 * h:128 * h + 128]
                half = half + pltpu.roll(half, 64, 1)
                for d in range(2):
                    send_c[4 * i + 2 * h + d] = jnp.where(
                        low_half[:64], half[128 * d:128 * d + 64], half[128 * d + 64:128 * d + 128]
                    ).astype(BF16)


    weights = (wg, wu)
    offsets = (0, 3, 1, 2)

    def q_copy(g, by):
        peer = SIDE * g + turn(x, by)
        return pltpu.make_async_remote_copy(
            src_ref=send_q.at[g], dst_ref=recv_q.at[ctx],
            send_sem=q_send.at[peer], recv_sem=q_recv.at[ctx],
            device_id={"ctx": peer}, device_id_type=MESH)

    def prepare(k):
        g = turn(z, offsets[k])
        block = rows[pl.ds(2 * g, 2)].reshape(128, 512).astype(F32)
        scaled[k] = (block * gain_ref[...]).astype(BF16)

    def squares_of(k):
        g = turn(z, offsets[k])
        block = rows[pl.ds(2 * g, 2)].reshape(128, 512).astype(F32)
        squares = block * block
        squares = (squares[:, :128] + squares[:, 128:256]) + (
            squares[:, 256:384] + squares[:, 384:])
        send_q[g] = jnp.broadcast_to(jnp.sum(squares.T, axis=0, keepdims=True), (8, 128))
        for by in range(1, SIDE):
            q_copy(g, by).start()

        @pl.when(g != y)
        def _():
            q_copy(g, 0).start()

        @pl.when(g == y)
        def _():
            recv_q[ctx] = send_q[g]

    first = (x, y)
    second = (y, x)

    def partial(k, h, c):
        g = turn(z, offsets[k])
        part = parts[h][c]
        result = jnp.dot(
            scaled[k], weights[h][:, STARTS[c]:STARTS[c] + CHUNKS[c]],
            preferred_element_type=F32)
        for b in range(SIDE):
            if h == 0:
                part[b, g] = result[32 * b:32 * b + 32]
            else:
                part[g, b] = result[32 * b:32 * b + 32]

    def near(h, step, by):
        along_x = (h == 0) == (step == 0)
        return turn(x, by) + SIDE * y if along_x else x + SIDE * turn(y, by)

    last = n - 1

    def link(h, c, kind):
        if kind == 4:
            src, dst, by = t1_out[h][c], t0_in[h][c], 2
        else:
            src, dst, by = ends(h, c, kind)
        i = (h * n + c) * 8 + kind
        return pltpu.make_async_remote_copy(
            src_ref=src, dst_ref=dst, send_sem=r_send.at[i], recv_sem=r_recv.at[i],
            device_id={"ctx": near(h, 0 if kind < 4 else 1, by)}, device_id_type=MESH)

    def ends(h, c, kind):
        return (
            (s1_out[h][c].at[pl.ds(0, 2)], s1p_in[h][c], 1),
            (s1_out[h][c].at[pl.ds(2, 2)], s1m_in[h][c], 3),
            (s2p_out[h][c], s2p_in[h][c], 1),
            (s2m_out[h][c], s2m_in[h][c], 3),
            (t1_out[h][c].at[pl.ds(0, 16)], t1p_in[h][c], 1),
            (t1_out[h][c].at[pl.ds(16, 16)], t1m_in[h][c], 3),
            (t2p_out[h][c], t2p_in[h][c], 1),
            (t2m_out[h][c], t2m_in[h][c], 3),
        )[kind]

    top, bottom = pl.ds(0, 16), pl.ds(16, 16)

    def step1(h, c):
        s1_out[h][c][...] = parts[h][c][turn(first[h], 2)].astype(BF16)
        link(h, c, 0).start()
        link(h, c, 1).start()

    def step2(h, c):
        part, ahead, behind = parts[h][c], turn(first[h], 1), turn(first[h], 3)
        link(h, c, 0).wait_recv()
        for b in range(2):
            s2p_out[h][c][b] = (part[ahead, b] + s1p_in[h][c][b].astype(F32)).astype(BF16)
            s2p_out[h][c][2 + b] = part[ahead, 2 + b].astype(BF16)
        link(h, c, 2).start()
        link(h, c, 1).wait_recv()
        for b in range(2):
            s2m_out[h][c][b] = part[behind, b].astype(BF16)
            s2m_out[h][c][2 + b] = (
                part[behind, 2 + b] + s1m_in[h][c][b].astype(F32)).astype(BF16)
        link(h, c, 3).start()

    def step3(h, c):
        part, f, s = parts[h][c], first[h], second[h]
        link(h, c, 2).wait_recv()
        link(h, c, 3).wait_recv()
        for b in range(SIDE):
            part[f, b] = (
                part[f, b] + s2p_in[h][c][b].astype(F32) + s2m_in[h][c][b].astype(F32))
        t1_out[h][c][...] = part[f, turn(s, 2)].astype(BF16)
        link(h, c, 4).start()
        t2p_out[h][c][...] = part[f, turn(s, 1)].astype(BF16)
        link(h, c, 6).start()
        t2m_out[h][c][...] = part[f, turn(s, 3)].astype(BF16)
        link(h, c, 7).start()

    def step4(h, c):
        part, f, s = parts[h][c], first[h], second[h]
        ahead, behind = turn(s, 1), turn(s, 3)
        link(h, c, 4).wait_recv()
        t2p_out[h][c][top] = (part[f, ahead, top] + t1p_in[h][c][...].astype(F32)).astype(BF16)
        t2p_out[h][c][bottom] = part[f, ahead, bottom].astype(BF16)
        link(h, c, 6).start()
        link(h, c, 5).wait_recv()
        t2m_out[h][c][top] = part[f, behind, top].astype(BF16)
        t2m_out[h][c][bottom] = (
            part[f, behind, bottom] + t1m_in[h][c][...].astype(F32)).astype(BF16)
        link(h, c, 7).start()

    def finish(c, scale):
        at = slice(STARTS[c], STARTS[c] + CHUNKS[c])
        for h, out in enumerate((gate_ref, up_ref)):
            total = parts[h][c][first[h], second[h]]
            link(h, c, 6).wait_recv()
            total += t2p_in[h][c][...].astype(F32)
            link(h, c, 7).wait_recv()
            total += t2m_in[h][c][...].astype(F32)
            if True:
                link(h, c, 4).wait_recv()
                total += t0_in[h][c][...].astype(F32)
            out[:, at] = total * scale

    def multiply(k):
        for c in range(n):
            for h in range(2):
                partial(k, h, c)

    mate = 1 - core
    before, after, across = (turn(z, by) * 2 + mate for by in (3, 1, 2))
    fill_tables(high, low, back)
    loads["acts"].wait()
    z_copy(4, other, 0, other, whole=True).wait_recv()
    prepare(0)
    squares_of(0)
    loads["wg"].wait()
    loads["wu"].wait()
    multiply(0)

    passed = []

    def forward(*copies):
        for copy in copies:
            copy.start()
            passed.append(copy)

    z_copy(0, left, 0, right).wait_recv()
    forward(z_copy(5, left, 0, right), z_copy(11, left, 0, right_mate))
    z_copy(1, right, 1, left).wait_recv()
    forward(z_copy(6, right, 1, left), z_copy(12, right, 1, left_mate))
    z_copy(2, left, 1, right).wait_recv()
    forward(z_copy(7, left, 0, other, whole=True))
    z_copy(3, right, 0, left).wait_recv()
    forward(z_copy(8, right, 0, other, whole=True))
    convolve()
    c_start()
    recv_c[ctx] = send_c[ctx]
    z_copy(7, before, 0, other, whole=True).wait_recv()
    prepare(1)
    squares_of(1)
    multiply(1)
    z_copy(8, after, 0, other, whole=True).wait_recv()
    prepare(2)
    squares_of(2)
    multiply(2)

    @pl.when(y != z)
    def _():
        for c in range(n):
            step1(1, c)

    z_copy(5, far, 0, right).wait_recv()
    z_copy(6, far, 1, left).wait_recv()
    z_copy(11, across, 0, right_mate).wait_recv()
    z_copy(12, across, 1, left_mate).wait_recv()
    prepare(3)
    for c in range(n):
        partial(3, 0, c)
        step1(0, c)
        partial(3, 1, c)

        @pl.when(y == z)
        def _(c=c):
            step1(1, c)

    squares_of(3)

    scale = None
    for c in range(n + 2):
        if c < n:
            step2(0, c)
            step2(1, c)
        if 0 <= c - 1 < n:
            step3(0, c - 1)
            step3(1, c - 1)
        if False:
            step4(0, c - 2)
            step4(1, c - 2)
        if c == 0:
            for copy in own + passed:
                copy.wait_send()
            u_drain()
        if c == 1:
            c_wait()
            loads["query"].wait()
            direct_gain = skip_ref[...].astype(F32)
            for i in range(GROUP // 2):
                at = slice(128 * i, 128 * i + 128)
                even = recv_c[2 * i].astype(F32)
                odd = recv_c[2 * i + 1].astype(F32)
                conv = jnp.concatenate(
                    (jnp.where(low_half[:64], even, pltpu.roll(odd, 64, 1)),
                     jnp.where(low_half[:64], pltpu.roll(even, 64, 1), odd)), axis=0)
                direct = direct_gain[at].reshape(1, 128) * mixed[:, at].astype(F32)
                gated_ref[:, at] = (
                    query[:, at].astype(F32) * (conv + direct)).astype(BF16)
            c_drain()
        if c == 2:
            @pl.loop(1, GROUP)
            def _(i):
                peer = lax.rem(ctx + i, GROUP)
                pltpu.make_async_remote_copy(
                    src_ref=send_q.at[0], dst_ref=recv_q.at[peer],
                    send_sem=q_send.at[peer], recv_sem=q_recv.at[peer],
                    device_id={"ctx": peer}, device_id_type=MESH).wait_recv()

            power = recv_q[0]
            for i in range(1, GROUP):
                power = power + recv_q[i]
            spread[...] = jnp.broadcast_to(power[0:1], (128, 128)).T
            mine = spread[pl.ds(pl.multiple_of(32 * x, 32), 32), :]
            scale = lax.rsqrt(mine[:, :1] / D + EPSILON)
            for k in range(SIDE):
                g = turn(z, offsets[k])
                for by in range(1, SIDE):
                    q_copy(g, by).wait_send()

                @pl.when(g != y)
                def _(g=g):
                    q_copy(g, 0).wait_send()
        if c >= 2:
            finish(c - 2, scale)
            for h in range(2):
                for kind in range(8):
                    if kind != 5:
                        link(h, c - 2, kind).wait_send()


def body(query_b, key_b, value_b, filter_b, skip_b, acts_a, gain_a, w_gate, w_up, grad_hidden):
    any_spec = pl.BlockSpec(memory_space=pl.ANY)
    vmem = pl.BlockSpec(memory_space=pltpu.VMEM)
    length, width = key_b.shape
    hidden = w_gate.shape[1]

    def per_chunk(*lead, kind=BF16):
        return [pltpu.VMEM(lead + (w,), kind) for w in CHUNKS] * 2

    scratch = [
        pltpu.VMEM((length, width), BF16),
        pltpu.VMEM((length, width), BF16),
        pltpu.VMEM((length, width), BF16),
        pltpu.VMEM((length, width), BF16),
        pltpu.VMEM(w_gate.shape, BF16),
        pltpu.VMEM(w_up.shape, BF16),
        pltpu.VMEM((2 * BLOCK, BLOCK), BF16),
        pltpu.VMEM((2 * BLOCK, BLOCK), BF16),
        pltpu.VMEM((BLOCK, 2 * BLOCK), BF16),
        pltpu.VMEM((length, width), BF16),
        pltpu.VMEM((GROUP, 128, 128), BF16),
        pltpu.VMEM((GROUP, 128, 128), BF16),
        pltpu.VMEM((8, 2 * BLOCK, 128), F32),
        pltpu.VMEM((8, 2 * BLOCK, 128), F32),
        pltpu.VMEM((8, 2 * BLOCK, 128), BF16),
        pltpu.VMEM((GROUP, 64, 128), BF16),
        pltpu.VMEM((GROUP, 64, 128), BF16),
        pltpu.VMEM((8, 64, 512), BF16),
        pltpu.VMEM((SIDE, 128, 512), BF16),
        pltpu.VMEM((SIDE, 8, 128), F32),
        pltpu.VMEM((GROUP, 8, 128), F32),
        pltpu.VMEM((128, 128), F32),
    ]
    scratch += per_chunk(SIDE, SIDE, 32, kind=F32)
    for lead in (
        (SIDE, 32), (2, 32), (2, 32), (SIDE, 32), (SIDE, 32), (SIDE, 32), (SIDE, 32),
        (32,), (16,), (16,), (32,), (32,), (32,), (32,),
    ):
        scratch += per_chunk(*lead)
    scratch += per_chunk(32)
    links = 2 * len(CHUNKS) * 8
    for size in (10, GROUP, GROUP, GROUP, GROUP, GROUP, GROUP, 13, 13, links, links):
        scratch.append(pltpu.SemaphoreType.DMA((size,)))
    gated, gate, up = pl.pallas_call(
        kernel,
        out_shape=(
            pltpu.VMEM((length, width), BF16),
            pltpu.VMEM(grad_hidden.shape, F32),
            pltpu.VMEM(grad_hidden.shape, F32),
        ),
        in_specs=[any_spec] * 4 + [vmem, any_spec, vmem] + [any_spec] * 2,
        out_specs=(vmem, vmem, vmem),
        scratch_shapes=scratch,
        compiler_params=pltpu.CompilerParams(
            collective_id=0, has_side_effects=True, vmem_limit_bytes=56 * 1024 * 1024),
        name="hyena",
    )(
        query_b, key_b, value_b, filter_b, skip_b, acts_a,
        gain_a.reshape(1, -1), w_gate, w_up,
    )
    sigma = jax.nn.sigmoid(gate)
    upstream = grad_hidden.astype(F32)
    grad_gate = (upstream * up * sigma * (1.0 + gate * (1.0 - sigma))).astype(BF16)
    grad_up = (upstream * gate * sigma).astype(BF16)
    return gated, grad_gate, grad_up


def solution(mesh):
    return jax.shard_map(
        body,
        mesh=mesh,
        in_specs=(
            P(("dp", "ctx"), "tp"),
            P(("dp", "ctx"), "tp"),
            P(("dp", "ctx"), "tp"),
            P("ctx", "tp"),
            P("tp"),
            P(("dp", "tp"), "ctx"),
            P("ctx"),
            P("ctx", "tp"),
            P("ctx", "tp"),
            P(("dp", "ctx"), "tp"),
        ),
        out_specs=(P(("dp", "ctx"), "tp"), P(("dp", "ctx"), "tp"), P(("dp", "ctx"), "tp")),
        check_vma=False,
    )
```
